256 devices in a mesh: row: 16 (over y, z_lo, core), col: 16 (over z_hi, x).
Axes of the slice: x: 4, y: 4, z: 8 (z_hi: 4, z_lo: 2; z = z_hi * 2 + z_lo), core: 2. Of those that a mesh axis runs over, the one named last changes fastest.
Arguments:
- layer_input: bfloat16 [2048, 12288], P('col', 'row'), may hold values from -6 to 6
- out_grad: bfloat16 [2048, 12288], P('col', 'row'), may hold values from -6 to 6
- preact: bfloat16 [2048, 16384], P('row', 'col'), may hold values from -6 to 6
- weight_in: bfloat16 [12288, 16384], P('row', 'col'), may hold values from -0.0546875 to 0.0546875
- weight_out: bfloat16 [16384, 12288], P('col', 'row'), may hold values from -0.046875 to 0.046875
Outputs:
- input_grad: bfloat16 [2048, 12288], P('col', 'row')
- weight_in_grad: float32 [12288, 16384], P('row', 'col')
- weight_out_grad: float32 [16384, 12288], P('col', 'row')
The draws below stay inside these ranges and needn't reach their ends.
All inputs are finite; a program needn't handle non-finite values.
Results may differ from the reference program's by a relative error of at most 0.019.
Values may be sent and summed in bfloat16 or wider, within the bound.
No kernel may reach another device: no remote copies, remote signals or barrier semaphores. Data moves between devices by JAX's collectives and lax.ppermute only.
A program may use at most 128 MiB of HBM per device.

```python
import math
import jax
import jax.numpy as jnp

D = 12288
FF = 16384
TOKENS = 2048


def spiked(entries, rng, source, target, parts, factor):
    def block_of(position):
        return (jnp.arange(entries.shape[position]) // (entries.shape[position] // parts)).reshape((-1,) + (1,) * (entries.ndim - 1 - position))

    first = jax.random.permutation(rng, parts)[block_of(target)]
    other_side = (block_of(target) + parts // 2) % parts
    return jnp.where((block_of(source) == first) | (block_of(source) == other_side), factor * entries, entries)


def level_of(key, extent, shards, smallest, high):
    def one(position, blocks):
        steps = jax.random.uniform(jax.random.fold_in(jax.random.fold_in(key, 6), position), (blocks,), jnp.float32, smallest / len(shards), high / len(shards))
        return jnp.repeat(jnp.exp(steps), extent[position] // blocks).reshape((-1,) + (1,) * (len(extent) - position - 1))

    factor_of = one(*shards[0])
    for cut in shards[1:]:
        factor_of = factor_of * one(*cut)
    return factor_of


def noise(key, extent, spread, bound, pieces=(), kind=jnp.bfloat16):
    factor_of = level_of(key, extent, pieces, -0.22, 0.18) if pieces else 1.0
    entries = jax.random.normal(key, extent, jnp.float32) * spread * factor_of
    return jnp.minimum(jnp.maximum(entries, -bound), bound).astype(kind)


def bell_draw_with(own_key, extent, deviation, bound, shards, heavy, held_as=jnp.bfloat16):
    entries = deviation * jax.random.normal(own_key, extent, jnp.float32)
    if shards:
        entries = entries * level_of(own_key, extent, shards, -0.22, 0.18)
    return jnp.clip(spiked(entries, jax.random.fold_in(own_key, 3), *heavy), -bound, bound).astype(held_as)


def setup_inputs(seed: int = 0) -> dict:
    splits = jax.random.split(jax.random.key(seed), 6)
    layer_input = noise(splits[0], (TOKENS, D), 1.0, 6.0, ((0, 16), (1, 16)))
    out_grad = bell_draw_with(splits[1], (TOKENS, D), 1.0, 6.0, ((0, 16), (1, 16)), (1, 0, 16, 2.0))
    preact = noise(splits[2], (TOKENS, FF), 1.5, 6.0, ((0, 16), (1, 16)))
    weight_in = noise(splits[3], (D, FF), D ** -0.5, 0.0546875, ((0, 16), (1, 16)))
    weight_out = noise(splits[4], (FF, D), FF ** -0.5, 0.046875, ((0, 16), (1, 16)))
    return {"layer_input": layer_input, "out_grad": out_grad, "preact": preact, "weight_in": weight_in, "weight_out": weight_out}


def gelu_parts(h):
    c = math.sqrt(2.0 / math.pi)
    t = jnp.tanh(c * (h + 0.044715 * h * h * h))
    value = 0.5 * h * (1.0 + t)
    slope = 0.5 * (1.0 + t) + 0.5 * h * (1.0 - t * t) * c * (1.0 + 3.0 * 0.044715 * h * h)
    return (value, slope)

def reference(layer_input, out_grad, preact, weight_in, weight_out):
    hidden = preact.astype(jnp.float32)
    value, slope = gelu_parts(hidden)
    activ = value.astype(jnp.bfloat16)
    grad_act = jnp.dot(out_grad, weight_out.T, preferred_element_type=jnp.float32)
    grad_pre = (grad_act * slope).astype(jnp.bfloat16)
    weight_out_grad = jnp.dot(activ.T, out_grad, preferred_element_type=jnp.float32)
    weight_in_grad = jnp.dot(layer_input.T, grad_pre, preferred_element_type=jnp.float32)
    input_grad = jnp.dot(grad_pre, weight_in.T, preferred_element_type=jnp.float32).astype(jnp.bfloat16)
    return (input_grad, weight_in_grad, weight_out_grad)
```

```python
import math

import jax
import jax.numpy as jnp
from jax import lax
from jax.sharding import PartitionSpec as P

BF = jnp.bfloat16
F32 = jnp.float32


def gelu_parts(h):
    c = math.sqrt(2.0 / math.pi)
    t = jnp.tanh(c * (h + 0.044715 * h * h * h))
    value = 0.5 * h * (1.0 + t)
    slope = 0.5 * (1.0 + t) + 0.5 * h * (1.0 - t * t) * c * (1.0 + 3.0 * 0.044715 * h * h)
    return (value, slope)


def token_contract(left, right):
    return lax.dot_general(left, right, (((0,), (0,)), ((), ())), preferred_element_type=F32)


def width_contract(left, right):
    return lax.dot_general(left, right, (((1,), (1,)), ((), ())), preferred_element_type=F32)


def move(v, axis, span, stride, step):
    def to(i):
        at = (i // stride) % span
        return i + (((at + step) % span) - at) * stride

    return lax.ppermute(v, axis, [(i, to(i)) for i in range(16)])


def along_x(v, d):
    return move(v, "col", 4, 1, d)


def along_zh(v, d):
    return move(v, "col", 4, 4, d)


def along_y(v, d):
    return move(v, "row", 4, 4, d)


def along_zl(v):
    return move(v, "row", 2, 2, 1)


def along_core(v):
    return move(v, "row", 2, 1, 1)


STEPS = (1, -1, 2)


def put(whole, piece, at, dim):
    return lax.dynamic_update_slice_in_dim(whole, jnp.expand_dims(piece, dim), at, dim)


def take(whole, at, dim):
    return lax.dynamic_index_in_dim(whole, at, dim, keepdims=False)


def gather4(shift, own, me, dim):
    shape = list(own.shape)
    shape.insert(dim, 4)
    whole = put(jnp.zeros(shape, own.dtype), own, me, dim)
    got = [(d, shift(own, d)) for d in STEPS]
    for d, piece in got:
        whole = put(whole, piece, (me - d) % 4, dim)
    return whole


def scatter4(shift, whole, me, dim):
    got = [shift(take(whole, (me + d) % 4, dim).astype(BF), d) for d in STEPS]
    total = take(whole, me, dim)
    for piece in got:
        total = total + piece.astype(F32)
    return total


def local(layer_input, out_grad, preact, weight_in, weight_out):
    col, row = lax.axis_index("col"), lax.axis_index("row")
    zh, x = col // 4, col % 4
    y, zl, core = row // 4, (row // 2) % 2, row % 2
    rows, width = out_grad.shape
    hidden = preact.shape[1]

    activ, slope = gelu_parts(preact.astype(F32))
    activ_panel = lax.all_gather(activ.astype(BF), "row", axis=0, tiled=True)
    input_panel = lax.all_gather(layer_input, "col", axis=0, tiled=True)

    by_z = gather4(along_zh, out_grad, zh, 0)
    og = gather4(along_x, by_z, x, 1)
    og_panel = og.reshape(16 * rows, width)
    og5 = og.reshape(4, 2, 2, rows, width)

    def grad_for(c):
        part = take(og5, c, 2).reshape(8 * rows, width)
        return width_contract(part, weight_out)

    away = along_core(grad_for(1 - core).astype(BF))
    mine = grad_for(core) + away.astype(F32)
    mine = mine.reshape(4, 2, rows, hidden)
    pair = scatter4(along_y, mine, y, 0)
    grad_act = take(pair, zl, 0) + along_zl(take(pair, 1 - zl, 0).astype(BF)).astype(F32)
    grad_pre = (grad_act * slope).astype(BF)

    other = along_zl(grad_pre)
    pair = put(put(jnp.zeros((2, rows, hidden), BF), grad_pre, zl, 0), other, 1 - zl, 0)
    half = gather4(along_y, pair, y, 0)
    rest = along_core(half)
    gp = put(put(jnp.zeros((4, 2, 2, rows, hidden), BF), half, core, 2), rest, 1 - core, 2)
    gp_panel = gp.reshape(16 * rows, hidden)

    partial = width_contract(gp_panel, weight_in).reshape(4, 4, rows, width)
    by_x = scatter4(along_x, partial, x, 1)
    input_grad = scatter4(along_zh, by_x, zh, 0).astype(BF)

    weight_out_grad = token_contract(activ_panel, og_panel)
    weight_in_grad = token_contract(input_panel, gp_panel)
    return (input_grad, weight_in_grad, weight_out_grad)


def solution(mesh):
    placed = (P("col", "row"), P("col", "row"), P("row", "col"), P("row", "col"), P("col", "row"))
    return jax.shard_map(
        local,
        mesh=mesh,
        in_specs=placed,
        out_specs=(P("col", "row"), P("row", "col"), P("col", "row")),
        check_vma=False,
    )
```

```python
import math

import jax
import jax.numpy as jnp
from jax import lax
from jax.sharding import PartitionSpec as P

BF = jnp.bfloat16
F32 = jnp.float32


def gelu_parts(h):
    c = math.sqrt(2.0 / math.pi)
    t = jnp.tanh(c * (h + 0.044715 * h * h * h))
    value = 0.5 * h * (1.0 + t)
    slope = 0.5 * (1.0 + t) + 0.5 * h * (1.0 - t * t) * c * (1.0 + 3.0 * 0.044715 * h * h)
    return (value, slope)


def token_contract(left, right):
    return lax.dot_general(left, right, (((0,), (0,)), ((), ())), preferred_element_type=F32)


def width_contract(left, right):
    return lax.dot_general(left, right, (((1,), (1,)), ((), ())), preferred_element_type=F32)


def move(v, axis, span, stride, step):
    def to(i):
        at = (i // stride) % span
        return i + (((at + step) % span) - at) * stride

    return lax.ppermute(v, axis, [(i, to(i)) for i in range(16)])


def along_x(v, d):
    return move(v, "col", 4, 1, d)


def along_zh(v, d):
    return move(v, "col", 4, 4, d)


def along_y(v, d):
    return move(v, "row", 4, 4, d)


def along_zl(v):
    return move(v, "row", 2, 2, 1)


def along_core(v):
    return move(v, "row", 2, 1, 1)


STEPS = (1, -1, 2)


def put(whole, piece, at, dim):
    return lax.dynamic_update_slice_in_dim(whole, jnp.expand_dims(piece, dim), at, dim)


def take(whole, at, dim):
    return lax.dynamic_index_in_dim(whole, at, dim, keepdims=False)


def gather4(shift, own, me, dim):
    shape = list(own.shape)
    shape.insert(dim, 4)
    whole = put(jnp.zeros(shape, own.dtype), own, me, dim)
    got = [(d, shift(own, d)) for d in STEPS]
    for d, piece in got:
        whole = put(whole, piece, (me - d) % 4, dim)
    return whole


def scatter4(shift, whole, me, dim):
    got = [shift(take(whole, (me + d) % 4, dim).astype(BF), d) for d in STEPS]
    total = take(whole, me, dim)
    for piece in got:
        total = total + piece.astype(F32)
    return total


def after(v, *others):
    return lax.optimization_barrier((v, *others))[0]


CHUNKS = 2


def local(layer_input, out_grad, preact, weight_in, weight_out):
    col, row = lax.axis_index("col"), lax.axis_index("row")
    zh, x = col // 4, col % 4
    y, zl, core = row // 4, (row // 2) % 2, row % 2
    width = out_grad.shape[1]
    hidden = preact.shape[1]
    n = out_grad.shape[0] // CHUNKS

    def part(v, k):
        return v[k * n : (k + 1) * n]

    def z_gather(k, tie):
        own = part(out_grad, k)
        return gather4(along_zh, after(own, *tie) if tie else own, zh, 0)

    def x_gather(by_z, tie):
        return gather4(along_x, after(by_z, *tie) if tie else by_z, x, 1)

    def core_sum(og):
        og5 = og.reshape(4, 2, 2, n, width)

        def grad_for(c):
            return width_contract(take(og5, c, 2).reshape(8 * n, width), weight_out)

        away = along_core(grad_for(1 - core).astype(BF))
        mine = grad_for(core) + away.astype(F32)
        return mine.reshape(4, 2, n, hidden)

    def z_pair_sum(pair):
        sent = pair.astype(BF)
        return sent.astype(F32) + along_zl(sent).astype(F32)

    def y_gather(grad_pre):
        return gather4(along_y, grad_pre, y, 0)

    def core_gather(half):
        whole = put(jnp.zeros((4, 2, 2, n, hidden), BF), half, core, 2)
        return put(whole, along_core(half), 1 - core, 2)

    def partials(gp):
        return width_contract(gp.reshape(16 * n, hidden), weight_in).reshape(4, 4, n, width)

    activ = gelu_parts(preact.astype(F32))[0].astype(BF)
    pre_pair = put(put(jnp.zeros((2,) + preact.shape, BF), preact, zl, 0), along_zl(preact), 1 - zl, 0)
    slope = gelu_parts(pre_pair.astype(F32))[1]

    bz0 = z_gather(0, ())
    bz1 = z_gather(1, ())
    activ0 = lax.all_gather(part(activ, 0), "row", axis=0, tiled=True)
    activ1 = lax.all_gather(part(activ, 1), "row", axis=0, tiled=True)
    og0 = x_gather(bz0, ())
    mine0 = core_sum(og0)
    og1 = x_gather(bz1, (og0,))
    pair0 = scatter4(along_y, mine0, y, 0)
    mine1 = core_sum(og1)
    input0 = lax.all_gather(after(part(layer_input, 0), og1), "col", axis=0, tiled=True)
    input1 = lax.all_gather(after(part(layer_input, 1), og1), "col", axis=0, tiled=True)
    act0 = z_pair_sum(pair0)
    gpre0 = (act0 * slope[:, :n]).astype(BF)
    pair1 = scatter4(along_y, mine1, y, 0)
    half0 = y_gather(gpre0)
    act1 = z_pair_sum(pair1)
    gpre1 = (act1 * slope[:, n:]).astype(BF)
    gp0 = core_gather(half0)
    part0 = partials(gp0)
    half1 = y_gather(gpre1)
    by_x0 = scatter4(along_x, part0, x, 1)
    gp1 = core_gather(half1)
    part1 = partials(gp1)
    out0 = scatter4(along_zh, by_x0, zh, 0).astype(BF)
    by_x1 = scatter4(along_x, part1, x, 1)
    out1 = scatter4(along_zh, by_x1, zh, 0).astype(BF)
    input_grad = jnp.concatenate([out0, out1], axis=0)

    weight_out_grad = token_contract(activ0, og0.reshape(16 * n, width))
    weight_out_grad = weight_out_grad + token_contract(activ1, og1.reshape(16 * n, width))
    weight_in_grad = token_contract(input0, gp0.reshape(16 * n, hidden))
    weight_in_grad = weight_in_grad + token_contract(input1, gp1.reshape(16 * n, hidden))
    return (input_grad, weight_in_grad, weight_out_grad)


def solution(mesh):
    placed = (P("col", "row"), P("col", "row"), P("row", "col"), P("row", "col"), P("col", "row"))
    return jax.shard_map(
        local,
        mesh=mesh,
        in_specs=placed,
        out_specs=(P("col", "row"), P("row", "col"), P("col", "row")),
        check_vma=False,
    )
```

```python
import math

import jax
import jax.numpy as jnp
from jax import lax
from jax.sharding import PartitionSpec as P

BF = jnp.bfloat16
F32 = jnp.float32


def gelu_parts(h):
    c = math.sqrt(2.0 / math.pi)
    t = jnp.tanh(c * (h + 0.044715 * h * h * h))
    value = 0.5 * h * (1.0 + t)
    slope = 0.5 * (1.0 + t) + 0.5 * h * (1.0 - t * t) * c * (1.0 + 3.0 * 0.044715 * h * h)
    return (value, slope)


def token_contract(left, right):
    return lax.dot_general(left, right, (((0,), (0,)), ((), ())), preferred_element_type=F32)


def width_contract(left, right):
    return lax.dot_general(left, right, (((1,), (1,)), ((), ())), preferred_element_type=F32)


def move(v, axis, span, stride, step):
    def to(i):
        at = (i // stride) % span
        return i + (((at + step) % span) - at) * stride

    return lax.ppermute(v, axis, [(i, to(i)) for i in range(16)])


def along_x(v, d):
    return move(v, "col", 4, 1, d)


def along_zh(v, d):
    return move(v, "col", 4, 4, d)


def along_y(v, d):
    return move(v, "row", 4, 4, d)


def along_zl(v):
    return move(v, "row", 2, 2, 1)


def along_core(v):
    return move(v, "row", 2, 1, 1)


STEPS = (1, -1, 2)


def put(whole, piece, at, dim):
    return lax.dynamic_update_slice_in_dim(whole, jnp.expand_dims(piece, dim), at, dim)


def take(whole, at, dim):
    return lax.dynamic_index_in_dim(whole, at, dim, keepdims=False)


def spread(own, copies, dim):
    shape = list(own.shape)
    shape.insert(dim, copies)
    return jnp.broadcast_to(jnp.expand_dims(own, dim), shape)


def gather4(shift, own, me, dim, hold=()):
    got = [(d, shift(own, d)) for d in STEPS]
    whole = after(spread(own, 4, dim), *hold)
    for d, piece in got:
        whole = put(whole, piece, (me - d) % 4, dim)
    return whole


def blocks_away(whole, me, dim):
    return [take(whole, (me + d) % 4, dim).astype(BF) for d in STEPS]


def scatter4(shift, whole, away, me, dim, hold=()):
    got = [shift(block, d) for block, d in zip(away, STEPS)]
    total = after(take(whole, me, dim), *hold)
    for piece in got:
        total = total + piece.astype(F32)
    return total


def pair2(own, other, me, dim):
    return put(spread(own, 2, dim), other, 1 - me, dim)


def after(v, *others):
    return lax.optimization_barrier((v, *others))[0] if others else v


CHUNKS = 2


def local(layer_input, out_grad, preact, weight_in, weight_out):
    col, row = lax.axis_index("col"), lax.axis_index("row")
    zh, x = col // 4, col % 4
    y, zl, core = row // 4, (row // 2) % 2, row % 2
    tokens, width = out_grad.shape
    hidden = preact.shape[1]
    n = tokens // CHUNKS

    def core_sum(og):
        og5 = og.reshape(2, 2, 4, n, width)

        def grad_for(c):
            return width_contract(take(og5, c, 1).reshape(8 * n, width), weight_out)

        away = along_core(grad_for(1 - core).astype(BF))
        mine = grad_for(core) + away.astype(F32)
        return mine.reshape(2, 4, n, hidden)

    def pre_grad(sent, k):
        grad_act = sent.astype(F32) + along_zl(sent).astype(F32)
        return (grad_act * slope[:, k * n : (k + 1) * n]).astype(BF)

    def partials(gp):
        return width_contract(gp.reshape(16 * n, hidden), weight_in).reshape(4, 4, n, width)

    def chunk_of(v, k):
        return v[:, :, k * n : (k + 1) * n].reshape(16 * n, v.shape[-1])

    bz0 = gather4(along_zh, out_grad[:n], zh, 0)
    activ = gelu_parts(preact.astype(F32))[0].astype(BF)
    activ_panel = lax.all_gather(activ, "row", axis=0, tiled=True)
    pre_pair = pair2(preact, along_zl(preact), zl, 0)
    slope = gelu_parts(pre_pair.astype(F32))[1]

    bz1 = gather4(along_zh, after(out_grad[n:], bz0), zh, 0)
    og0 = gather4(along_x, bz0, x, 0, hold=(bz1, slope))
    input_z = gather4(along_zh, after(layer_input, bz1), zh, 0)
    mine0 = core_sum(og0)
    away0 = blocks_away(mine0, y, 1)
    og1 = gather4(along_x, after(bz1, og0), x, 0, hold=(*away0, input_z, activ_panel))
    input_panel = lax.all_gather(
        after(input_z, og1), "col", axis=0, tiled=False,
        axis_index_groups=[[z * 4 + i for i in range(4)] for z in range(4)],
    )
    activ_x = activ_panel.reshape(4, 4, tokens, hidden).transpose(1, 0, 2, 3)

    def out_term(k, og, *first):
        return token_contract(after(chunk_of(activ_x, k), *first), og.reshape(16 * n, width))

    def in_term(k, gp, *first):
        return token_contract(after(chunk_of(input_panel, k), *first), gp.reshape(16 * n, hidden))

    mine1 = core_sum(og1)
    away1 = blocks_away(mine1, y, 1)
    pair0 = scatter4(along_y, mine0, away0, y, 1, hold=tuple(away1))
    gpre0 = pre_grad(pair0.astype(BF), 0)
    pair1 = scatter4(along_y, mine1, away1, y, 1, hold=(gpre0,))
    sent1 = pair1.astype(BF)
    weight_out_grad = out_term(0, og0, sent1)
    gpre1 = pre_grad(sent1, 1)
    half0 = gather4(along_y, gpre0, y, 1, hold=(gpre1, weight_out_grad, input_panel))
    gp0 = pair2(half0, along_core(half0), core, 1)
    part0 = partials(gp0)
    far0 = blocks_away(part0, x, 0)
    weight_out_grad = weight_out_grad + out_term(1, og1, *far0)
    half1 = gather4(along_y, after(gpre1, half0), y, 1, hold=(*far0, weight_out_grad))
    gp1 = pair2(half1, along_core(half1), core, 1)
    part1 = partials(gp1)
    far1 = blocks_away(part1, x, 0)
    weight_in_grad = in_term(0, gp0, *far1)
    by_x0 = scatter4(along_x, part0, far0, x, 0, hold=(*far1, weight_in_grad))
    up0 = blocks_away(by_x0, zh, 0)
    weight_in_grad = weight_in_grad + in_term(1, gp1, *up0)
    out0 = scatter4(along_zh, by_x0, up0, zh, 0).astype(BF)
    by_x1 = scatter4(along_x, part1, far1, x, 0, hold=(weight_in_grad,))
    up1 = blocks_away(by_x1, zh, 0)
    out1 = scatter4(along_zh, by_x1, up1, zh, 0).astype(BF)
    input_grad = jnp.concatenate([out0, out1], axis=0)
    return (input_grad, weight_in_grad, weight_out_grad)


def solution(mesh):
    placed = (P("col", "row"), P("col", "row"), P("row", "col"), P("row", "col"), P("col", "row"))
    return jax.shard_map(
        local,
        mesh=mesh,
        in_specs=placed,
        out_specs=(P("col", "row"), P("row", "col"), P("col", "row")),
        check_vma=False,
    )
```

```python
import math

import jax
import jax.numpy as jnp
from jax import lax
from jax.sharding import PartitionSpec as P

BF = jnp.bfloat16
F32 = jnp.float32


def gelu_parts(h):
    c = math.sqrt(2.0 / math.pi)
    t = jnp.tanh(c * (h + 0.044715 * h * h * h))
    value = 0.5 * h * (1.0 + t)
    slope = 0.5 * (1.0 + t) + 0.5 * h * (1.0 - t * t) * c * (1.0 + 3.0 * 0.044715 * h * h)
    return (value, slope)


def token_contract(left, right):
    return lax.dot_general(left, right, (((0,), (0,)), ((), ())), preferred_element_type=F32)


def width_contract(left, right):
    return lax.dot_general(left, right, (((1,), (1,)), ((), ())), preferred_element_type=F32)


def move(v, axis, span, stride, step):
    def to(i):
        at = (i // stride) % span
        return i + (((at + step) % span) - at) * stride

    return lax.ppermute(v, axis, [(i, to(i)) for i in range(16)])


def swap(v, axis, bit):
    return lax.ppermute(v, axis, [(i, i ^ bit) for i in range(16)])


def along_x(v, d):
    return move(v, "col", 4, 1, d)


def along_zh(v, d):
    return move(v, "col", 4, 4, d)


def along_y(v, d):
    return move(v, "row", 4, 4, d)


def along_zl(v):
    return move(v, "row", 2, 2, 1)


def along_core(v):
    return move(v, "row", 2, 1, 1)


STEPS = (1, -1, 2)


def put(whole, piece, at, dim):
    return lax.dynamic_update_slice_in_dim(whole, jnp.expand_dims(piece, dim), at, dim)


def take(whole, at, dim):
    return lax.dynamic_index_in_dim(whole, at, dim, keepdims=False)


def spread(own, copies, dim):
    shape = list(own.shape)
    shape.insert(dim, copies)
    return jnp.broadcast_to(jnp.expand_dims(own, dim), shape)


def gather4(shift, own, me, dim, hold=()):
    got = [(d, shift(own, d)) for d in STEPS]
    whole = after(spread(own, 4, dim), *hold)
    for d, piece in got:
        whole = put(whole, piece, (me - d) % 4, dim)
    return whole


def blocks_away(whole, me, dim):
    return [take(whole, (me + d) % 4, dim).astype(BF) for d in STEPS]


def scatter4(shift, whole, away, me, dim, hold=()):
    got = [shift(block, d) for block, d in zip(away, STEPS)]
    total = after(take(whole, me, dim), *hold)
    for piece in got:
        total = total + piece.astype(F32)
    return total


def pair2(own, other, me, dim, hold=()):
    return put(after(spread(own, 2, dim), *hold), other, 1 - me, dim)


def after(v, *others):
    return lax.optimization_barrier((v, *others))[0] if others else v


CHUNKS = 2


def local(layer_input, out_grad, preact, weight_in, weight_out):
    col, row = lax.axis_index("col"), lax.axis_index("row")
    zh, x = col // 4, col % 4
    y, zl, core = row // 4, (row // 2) % 2, row % 2
    tokens, width = out_grad.shape
    hidden = preact.shape[1]
    n = tokens // CHUNKS

    def core_sum(og):
        og5 = og.reshape(2, 2, 4, n, width)

        def grad_for(c):
            return width_contract(take(og5, c, 1).reshape(8 * n, width), weight_out)

        away = along_core(grad_for(1 - core).astype(BF))
        mine = grad_for(core) + away.astype(F32)
        return mine.reshape(2, 4, n, hidden)

    def pre_grad(sent, k):
        grad_act = sent.astype(F32) + along_zl(sent).astype(F32)
        return (grad_act * slope[:, k * n : (k + 1) * n]).astype(BF)

    def partials(gp):
        return width_contract(gp.reshape(16 * n, hidden), weight_in).reshape(4, 4, n, width)

    def chunk_of(v, k):
        return v[:, :, k * n : (k + 1) * n].reshape(16 * n, v.shape[-1])

    by_z = gather4(along_zh, out_grad, zh, 0)
    activ = gelu_parts(preact.astype(F32))[0].astype(BF)
    activ_panel = lax.all_gather(activ, "row", axis=0, tiled=True)
    pre_pair = pair2(preact, along_zl(preact), zl, 0)
    slope = gelu_parts(pre_pair.astype(F32))[1]

    low = pair2(layer_input, swap(after(layer_input, by_z), "col", 4), zh % 2, 0)
    og0 = gather4(along_x, by_z[:, :n], x, 0, hold=(slope, low))
    mine0 = core_sum(og0)
    away0 = blocks_away(mine0, y, 1)
    input_z = pair2(low, swap(low, "col", 8), zh // 2, 0, hold=tuple(away0))
    input_z = input_z.reshape(4, tokens, width)
    og1 = gather4(along_x, after(by_z[:, n:], og0), x, 0, hold=(*away0, activ_panel, input_z))
    input_panel = lax.all_gather(
        after(input_z, og1), "col", axis=0, tiled=False,
        axis_index_groups=[[z * 4 + i for i in range(4)] for z in range(4)],
    )
    activ_x = activ_panel.reshape(4, 4, tokens, hidden).transpose(1, 0, 2, 3)

    def out_term(k, og, *first):
        return token_contract(after(chunk_of(activ_x, k), *first), og.reshape(16 * n, width))

    def in_term(k, gp, *first):
        return token_contract(after(chunk_of(input_panel, k), *first), gp.reshape(16 * n, hidden))

    mine1 = core_sum(og1)
    away1 = blocks_away(mine1, y, 1)
    pair0 = scatter4(along_y, mine0, away0, y, 1, hold=tuple(away1))
    gpre0 = pre_grad(pair0.astype(BF), 0)
    pair1 = scatter4(along_y, mine1, [after(v, pair0) for v in away1], y, 1, hold=(gpre0,))
    sent1 = pair1.astype(BF)
    weight_out_grad = out_term(0, og0, sent1)
    gpre1 = pre_grad(sent1, 1)
    half0 = gather4(along_y, after(gpre0, pair1), y, 1, hold=(gpre1, weight_out_grad, input_panel))
    gp0 = pair2(half0, along_core(half0), core, 1)
    part0 = partials(gp0)
    far0 = blocks_away(part0, x, 0)
    half1 = gather4(along_y, after(gpre1, half0), y, 1, hold=tuple(far0))
    gp1 = pair2(half1, along_core(half1), core, 1)
    part1 = partials(gp1)
    far1 = blocks_away(part1, x, 0)
    weight_out_grad = weight_out_grad + out_term(1, og1, *far1)
    weight_in_grad = in_term(0, gp0, *far1)
    by_x0 = scatter4(along_x, part0, far0, x, 0, hold=(*far1, weight_out_grad, weight_in_grad))
    up0 = blocks_away(by_x0, zh, 0)
    weight_in_grad = weight_in_grad + in_term(1, gp1, *up0)
    out0 = scatter4(along_zh, by_x0, up0, zh, 0).astype(BF)
    by_x1 = scatter4(along_x, part1, [after(v, by_x0) for v in far1], x, 0, hold=(weight_in_grad,))
    up1 = blocks_away(by_x1, zh, 0)
    out1 = scatter4(along_zh, by_x1, up1, zh, 0).astype(BF)
    input_grad = jnp.concatenate([out0, out1], axis=0)
    return (input_grad, weight_in_grad, weight_out_grad)


def solution(mesh):
    placed = (P("col", "row"), P("col", "row"), P("row", "col"), P("row", "col"), P("col", "row"))
    return jax.shard_map(
        local,
        mesh=mesh,
        in_specs=placed,
        out_specs=(P("col", "row"), P("row", "col"), P("col", "row")),
        check_vma=False,
    )
```

```python
import math

import jax
import jax.numpy as jnp
from jax import lax
from jax.sharding import PartitionSpec as P

BF = jnp.bfloat16
F32 = jnp.float32


def gelu_parts(h):
    c = math.sqrt(2.0 / math.pi)
    t = jnp.tanh(c * (h + 0.044715 * h * h * h))
    value = 0.5 * h * (1.0 + t)
    slope = 0.5 * (1.0 + t) + 0.5 * h * (1.0 - t * t) * c * (1.0 + 3.0 * 0.044715 * h * h)
    return (value, slope)


def token_contract(left, right):
    return lax.dot_general(left, right, (((0,), (0,)), ((), ())), preferred_element_type=F32)


def width_contract(left, right):
    return lax.dot_general(left, right, (((1,), (1,)), ((), ())), preferred_element_type=F32)


def move(v, axis, span, stride, step):
    def to(i):
        at = (i // stride) % span
        return i + (((at + step) % span) - at) * stride

    return lax.ppermute(v, axis, [(i, to(i)) for i in range(16)])


def swap(v, axis, bit):
    return lax.ppermute(v, axis, [(i, i ^ bit) for i in range(16)])


def along_x(v, d):
    return move(v, "col", 4, 1, d)


def along_zh(v, d):
    return move(v, "col", 4, 4, d)


def along_y(v, d):
    return move(v, "row", 4, 4, d)


def along_zl(v):
    return move(v, "row", 2, 2, 1)


def along_core(v):
    return move(v, "row", 2, 1, 1)


STEPS = (1, -1, 2)


def gray(i):
    return i ^ (i // 2)


def put(whole, piece, at, dim):
    return lax.dynamic_update_slice_in_dim(whole, jnp.expand_dims(piece, dim), at, dim)


def take(whole, at, dim):
    return lax.dynamic_index_in_dim(whole, at, dim, keepdims=False)


def spread(own, copies, dim):
    shape = list(own.shape)
    shape.insert(dim, copies)
    return jnp.broadcast_to(jnp.expand_dims(own, dim), shape)


def gather4(shift, own, me, dim, hold=()):
    got = [(d, shift(own, d)) for d in STEPS]
    whole = after(spread(own, 4, dim), *hold)
    for d, piece in got:
        whole = put(whole, piece, (me - d) % 4, dim)
    return whole


def blocks_away(whole, me, dim):
    return [take(whole, (me + d) % 4, dim).astype(BF) for d in STEPS]


def scatter4(shift, whole, away, me, dim, hold=()):
    got = [shift(block, d) for block, d in zip(away, STEPS)]
    total = after(take(whole, me, dim), *hold)
    for piece in got:
        total = total + piece.astype(F32)
    return total


def pair2(own, other, me, dim, hold=()):
    return put(after(spread(own, 2, dim), *hold), other, 1 - me, dim)


def after(v, *others):
    return lax.optimization_barrier((v, *others))[0] if others else v


CHUNKS = 2


def local(layer_input, out_grad, preact, weight_in, weight_out):
    col, row = lax.axis_index("col"), lax.axis_index("row")
    zh, x = col // 4, col % 4
    y, zl, core = row // 4, (row // 2) % 2, row % 2
    tokens, width = out_grad.shape
    hidden = preact.shape[1]
    n = tokens // CHUNKS

    def core_sum(og):
        og5 = og.reshape(2, 2, 4, n, width)

        def grad_for(c):
            return width_contract(take(og5, c, 1).reshape(8 * n, width), weight_out)

        away = along_core(grad_for(1 - core).astype(BF))
        mine = grad_for(core) + away.astype(F32)
        return mine.reshape(2, 4, n, hidden)

    def y_first(mine):
        def send(half, step):
            two = [take(mine[half], y ^ step, 0), take(mine[half], y ^ 2, 0)]
            return jnp.stack(two).astype(BF)

        return send(0, 1), send(1, 3)

    def y_second(mine, sends):
        got = swap(sends[0], "row", 4).astype(F32), swap(sends[1], "row", 12).astype(F32)
        kept = [take(mine[half], y, 0) + got[half][0] for half in (0, 1)]
        passed = take(mine[0], y ^ 3, 0) + got[0][1], take(mine[1], y ^ 1, 0) + got[1][1]
        return kept, [v.astype(BF) for v in passed]

    def y_last(kept, sends, hold=()):
        kept = [after(v, *hold) for v in kept]
        total = kept[0] + swap(sends[0], "row", 12).astype(F32), kept[1] + swap(sends[1], "row", 4).astype(F32)
        return jnp.stack(total).astype(BF)

    def y_gather(share, hold=()):
        low, high = gray(y) % 2, gray(y) // 2
        one = pair2(share[0], swap(share[0], "row", 4), low, 0)
        two = pair2(share[1], swap(share[1], "row", 12), high, 0)
        one = pair2(one, swap(one, "row", 12), high, 0, hold=hold)
        two = pair2(two, swap(two, "row", 4), low, 1, hold=hold)
        return jnp.stack([one, two]).reshape(2, 4, n, hidden)

    def pre_grad(sent, k):
        grad_act = sent.astype(F32) + along_zl(sent).astype(F32)
        return (grad_act * slope[:, k * n : (k + 1) * n]).astype(BF)

    def partials(gp):
        return width_contract(gp.reshape(16 * n, hidden), weight_in).reshape(4, 4, n, width)

    def up_blocks(by_x):
        return [take(by_x, gray((zh + d) % 4), 0).astype(BF) for d in STEPS]

    def chunk_of(v, k):
        return v[:, :, k * n : (k + 1) * n].reshape(16 * n, v.shape[-1])

    by_z = gather4(along_zh, out_grad, zh, 0)
    activ = gelu_parts(preact.astype(F32))[0].astype(BF)
    activ_panel = lax.all_gather(activ, "row", axis=0, tiled=True)
    pre_pair = pair2(preact, along_zl(preact), zl, 0)
    slope = gelu_parts(pre_pair.astype(F32))[1]

    low = pair2(layer_input, swap(after(layer_input, by_z), "col", 4), gray(zh) % 2, 0)
    og0 = gather4(along_x, by_z[:, :n], x, 0, hold=(slope, low))
    mine0 = core_sum(og0)
    kept0, sends0 = y_second(mine0, y_first(mine0))
    og1 = gather4(along_x, after(by_z[:, n:], og0), x, 0, hold=(*sends0, activ_panel))
    activ_x = activ_panel.reshape(4, 4, tokens, hidden).transpose(1, 0, 2, 3)

    def out_term(k, og, *first):
        return token_contract(after(chunk_of(activ_x, k), *first), og.reshape(16 * n, width))

    mine1 = core_sum(og1)
    sent0 = y_last(kept0, sends0)
    first1 = [after(v, sent0) for v in y_first(mine1)]
    kept1, sends1 = y_second(mine1, first1)
    gpre0 = pre_grad(sent0, 0)
    sent1 = y_last(kept1, sends1, hold=(gpre0,))
    high = swap(after(low, og1), "col", 12)
    input_z = pair2(low, high, gray(zh) // 2, 0, hold=tuple(sends1)).reshape(4, tokens, width)
    input_panel = lax.all_gather(
        input_z, "col", axis=0, tiled=False,
        axis_index_groups=[[z * 4 + i for i in range(4)] for z in range(4)],
    )

    def in_term(k, gp, *first):
        return token_contract(after(chunk_of(input_panel, k), *first), gp.reshape(16 * n, hidden))

    weight_out_grad = out_term(0, og0, sent1)
    gpre1 = pre_grad(sent1, 1)
    half0 = y_gather(after(gpre0, sent1), hold=(gpre1, weight_out_grad))
    gp0 = pair2(half0, along_core(half0), core, 1)
    part0 = partials(gp0)
    far0 = blocks_away(part0, x, 0)
    half1 = y_gather(after(gpre1, half0), hold=tuple(far0))
    gp1 = pair2(half1, along_core(half1), core, 1)
    part1 = partials(gp1)
    far1 = blocks_away(part1, x, 0)
    weight_out_grad = weight_out_grad + out_term(1, og1, *far1)
    weight_in_grad = in_term(0, gp0, *far1)
    by_x0 = scatter4(along_x, part0, far0, x, 0, hold=(*far1, weight_out_grad, weight_in_grad))
    up0 = up_blocks(by_x0)
    weight_in_grad = weight_in_grad + in_term(1, gp1, *up0)
    out0 = scatter4(along_zh, by_x0, up0, gray(zh), 0).astype(BF)
    by_x1 = scatter4(along_x, part1, [after(v, by_x0) for v in far1], x, 0, hold=(weight_in_grad,))
    up1 = up_blocks(by_x1)
    out1 = scatter4(along_zh, by_x1, up1, gray(zh), 0).astype(BF)
    input_grad = jnp.concatenate([out0, out1], axis=0)
    return (input_grad, weight_in_grad, weight_out_grad)


def solution(mesh):
    placed = (P("col", "row"), P("col", "row"), P("row", "col"), P("row", "col"), P("col", "row"))
    return jax.shard_map(
        local,
        mesh=mesh,
        in_specs=placed,
        out_specs=(P("col", "row"), P("row", "col"), P("col", "row")),
        check_vma=False,
    )
```

```python
import math

import jax
import jax.numpy as jnp
from jax import lax
from jax.sharding import PartitionSpec as P

BF = jnp.bfloat16
F32 = jnp.float32


def gelu_parts(h):
    c = math.sqrt(2.0 / math.pi)
    t = jnp.tanh(c * (h + 0.044715 * h * h * h))
    value = 0.5 * h * (1.0 + t)
    slope = 0.5 * (1.0 + t) + 0.5 * h * (1.0 - t * t) * c * (1.0 + 3.0 * 0.044715 * h * h)
    return (value, slope)


def token_contract(left, right):
    return lax.dot_general(left, right, (((0,), (0,)), ((), ())), preferred_element_type=F32)


def width_contract(left, right):
    return lax.dot_general(left, right, (((1,), (1,)), ((), ())), preferred_element_type=F32)


def move(v, axis, span, stride, step):
    def to(i):
        at = (i // stride) % span
        return i + (((at + step) % span) - at) * stride

    return lax.ppermute(v, axis, [(i, to(i)) for i in range(16)])


def swap(v, axis, bit):
    return lax.ppermute(v, axis, [(i, i ^ bit) for i in range(16)])


def around_x(v, first):
    def to(i):
        return i ^ (1 if (i // 16 % 2 == 0) == first else 3)

    return lax.ppermute(v, ("row", "col"), [(i, to(i)) for i in range(256)])


def along_x(v, d):
    return move(v, "col", 4, 1, d)


def along_zh(v, d):
    return move(v, "col", 4, 4, d)


def along_y(v, d):
    return move(v, "row", 4, 4, d)


def along_zl(v):
    return move(v, "row", 2, 2, 1)


def along_core(v):
    return move(v, "row", 2, 1, 1)


STEPS = (1, -1, 2)


def put(whole, piece, at, dim):
    return lax.dynamic_update_slice_in_dim(whole, jnp.expand_dims(piece, dim), at, dim)


def take(whole, at, dim):
    return lax.dynamic_index_in_dim(whole, at, dim, keepdims=False)


def spread(own, copies, dim):
    shape = list(own.shape)
    shape.insert(dim, copies)
    return jnp.broadcast_to(jnp.expand_dims(own, dim), shape)


def gather4(shift, own, me, dim, hold=()):
    got = [(d, shift(own, d)) for d in STEPS]
    whole = after(spread(own, 4, dim), *hold)
    for d, piece in got:
        whole = put(whole, piece, (me - d) % 4, dim)
    return whole


def blocks_away(whole, me, dim):
    return [take(whole, (me + d) % 4, dim).astype(BF) for d in STEPS]


def scatter4(shift, whole, away, me, dim, hold=()):
    got = [shift(block, d) for block, d in zip(away, STEPS)]
    total = after(take(whole, me, dim), *hold)
    for piece in got:
        total = total + piece.astype(F32)
    return total


def pair2(own, other, me, dim, hold=()):
    return put(after(spread(own, 2, dim), *hold), other, 1 - me, dim)


def after(v, *others):
    return lax.optimization_barrier((v, *others))[0] if others else v


CHUNKS = 2


def local(layer_input, out_grad, preact, weight_in, weight_out):
    col, row = lax.axis_index("col"), lax.axis_index("row")
    zh, x = col // 4, col % 4
    y, zl, core = row // 4, (row // 2) % 2, row % 2
    tokens, width = out_grad.shape
    hidden = preact.shape[1]
    n = tokens // CHUNKS

    def x_gather(own, hold):
        first = 1 + 2 * core
        near = around_x(own, True)
        far = around_x(jnp.stack([own, near]), False)
        whole = put(after(spread(own, 4, 0), *hold), near, x ^ first, 0)
        return put(put(whole, far[0], x ^ (4 - first), 0), far[1], x ^ 2, 0)

    def core_sum(og):
        og5 = og.reshape(2, 2, 4, tokens, width)

        def grad_for(c):
            return width_contract(take(og5, c, 1).reshape(8 * tokens, width), weight_out)

        away = along_core(grad_for(1 - core).astype(BF))
        mine = grad_for(core) + away.astype(F32)
        return mine.reshape(2, 4, tokens, hidden)

    def token_sum(left, right, *first):
        left = after(left.reshape(2, 8 * tokens, left.shape[-1]), *first)
        right = right.reshape(2, 8 * tokens, right.shape[-1])
        return token_contract(left[0], right[0]) + token_contract(left[1], right[1])

    by_z = gather4(along_zh, out_grad, zh, 0)
    activ = gelu_parts(preact.astype(F32))[0].astype(BF)
    activ_panel = lax.all_gather(activ, "row", axis=0, tiled=True)
    pre_pair = pair2(preact, along_zl(preact), zl, 0)
    slope = gelu_parts(pre_pair.astype(F32))[1]

    low = pair2(layer_input, swap(after(layer_input, by_z), "col", 4), zh % 2, 0)
    input_z = pair2(low, swap(low, "col", 12), zh // 2, 0)
    og = x_gather(by_z, (input_z, activ_panel))
    og, slope = lax.optimization_barrier((og, slope))
    mine = core_sum(og)
    away = blocks_away(mine, y, 1)
    input_panel = lax.all_gather(
        input_z.reshape(4, tokens, width), "col", axis=0, tiled=False,
        axis_index_groups=[[z * 4 + i for i in range(4)] for z in range(4)],
    )
    activ_x = after(activ_panel, *away).reshape(4, 4, tokens, hidden).transpose(1, 0, 2, 3)
    weight_out_grad = token_sum(activ_x, og)
    pair = scatter4(along_y, mine, away, y, 1, hold=(weight_out_grad,))
    sent = pair.astype(BF)
    grad_act = sent.astype(F32) + along_zl(sent).astype(F32)
    half = gather4(along_y, (grad_act * slope).astype(BF), y, 1, hold=(input_panel,))
    gp = pair2(half, along_core(half), core, 1)
    part = width_contract(gp.reshape(16 * tokens, hidden), weight_in).reshape(4, 4, tokens, width)
    part0, part1 = part[:, :, :n], part[:, :, n:]
    far0 = blocks_away(part0, x, 0)
    far1 = blocks_away(part1, x, 0)
    weight_in_grad = token_sum(input_panel, gp, *far1)
    by_x0 = scatter4(along_x, part0, far0, x, 0, hold=(weight_in_grad,))
    up0 = blocks_away(by_x0, zh, 0)
    out0 = scatter4(along_zh, by_x0, up0, zh, 0).astype(BF)
    by_x1 = scatter4(along_x, part1, [after(v, by_x0) for v in far1], x, 0)
    up1 = blocks_away(by_x1, zh, 0)
    out1 = scatter4(along_zh, by_x1, up1, zh, 0).astype(BF)
    input_grad = jnp.concatenate([out0, out1], axis=0)
    return (input_grad, weight_in_grad, weight_out_grad)


def solution(mesh):
    placed = (P("col", "row"), P("col", "row"), P("row", "col"), P("row", "col"), P("col", "row"))
    return jax.shard_map(
        local,
        mesh=mesh,
        in_specs=placed,
        out_specs=(P("col", "row"), P("row", "col"), P("col", "row")),
        check_vma=False,
    )
```

```python
import math

import jax
import jax.numpy as jnp
from jax import lax
from jax.sharding import PartitionSpec as P

BF = jnp.bfloat16
F32 = jnp.float32


def gelu_parts(h):
    c = math.sqrt(2.0 / math.pi)
    t = jnp.tanh(c * (h + 0.044715 * h * h * h))
    value = 0.5 * h * (1.0 + t)
    slope = 0.5 * (1.0 + t) + 0.5 * h * (1.0 - t * t) * c * (1.0 + 3.0 * 0.044715 * h * h)
    return (value, slope)


def token_contract(left, right):
    return lax.dot_general(left, right, (((0,), (0,)), ((), ())), preferred_element_type=F32)


def width_contract(left, right):
    return lax.dot_general(left, right, (((1,), (1,)), ((), ())), preferred_element_type=F32)


def move(v, axis, span, stride, step):
    def to(i):
        at = (i // stride) % span
        return i + (((at + step) % span) - at) * stride

    return lax.ppermute(v, axis, [(i, to(i)) for i in range(16)])


def swap(v, axis, bit):
    return lax.ppermute(v, axis, [(i, i ^ bit) for i in range(16)])


def around_x(v, first):
    def to(i):
        return i ^ (1 if (i // 16 % 2 == 0) == first else 3)

    return lax.ppermute(v, ("row", "col"), [(i, to(i)) for i in range(256)])


def around_y(v, first):
    def to(i):
        return i ^ (4 if (i % 2 == 0) == first else 12)

    return lax.ppermute(v, "row", [(i, to(i)) for i in range(16)])


def along_x(v, d):
    return move(v, "col", 4, 1, d)


def along_zh(v, d):
    return move(v, "col", 4, 4, d)


def along_y(v, d):
    return move(v, "row", 4, 4, d)


def along_zl(v):
    return move(v, "row", 2, 2, 1)


def along_core(v):
    return move(v, "row", 2, 1, 1)


STEPS = (1, -1, 2)


def put(whole, piece, at, dim):
    return lax.dynamic_update_slice_in_dim(whole, jnp.expand_dims(piece, dim), at, dim)


def take(whole, at, dim):
    return lax.dynamic_index_in_dim(whole, at, dim, keepdims=False)


def spread(own, copies, dim):
    shape = list(own.shape)
    shape.insert(dim, copies)
    return jnp.broadcast_to(jnp.expand_dims(own, dim), shape)


def gather4(shift, own, me, dim, hold=()):
    got = [(d, shift(own, d)) for d in STEPS]
    whole = after(spread(own, 4, dim), *hold)
    for d, piece in got:
        whole = put(whole, piece, (me - d) % 4, dim)
    return whole


def place4(own, near, far, me, core, dim, hold=()):
    first = 1 + 2 * core
    whole = put(after(spread(own, 4, dim), *hold), near, me ^ first, dim)
    return put(put(whole, far[0], me ^ (4 - first), dim), far[1], me ^ 2, dim)


def blocks_away(whole, me, dim):
    return [take(whole, (me + d) % 4, dim).astype(BF) for d in STEPS]


def scatter4(shift, whole, away, me, dim, hold=()):
    got = [shift(block, d) for block, d in zip(away, STEPS)]
    total = after(take(whole, me, dim), *hold)
    for piece in got:
        total = total + piece.astype(F32)
    return total


def pair2(own, other, me, dim, hold=()):
    return put(after(spread(own, 2, dim), *hold), other, 1 - me, dim)


def after(v, *others):
    return lax.optimization_barrier((v, *others))[0] if others else v


CHUNKS = 2


def local(layer_input, out_grad, preact, weight_in, weight_out):
    col, row = lax.axis_index("col"), lax.axis_index("row")
    zh, x = col // 4, col % 4
    y, zl, core = row // 4, (row // 2) % 2, row % 2
    tokens, width = out_grad.shape
    hidden = preact.shape[1]
    n = tokens // CHUNKS

    def core_sum(og):
        og5 = og.reshape(2, 2, 4, n, width)

        def grad_for(c):
            return width_contract(take(og5, c, 1).reshape(8 * n, width), weight_out)

        away = along_core(grad_for(1 - core).astype(BF))
        mine = grad_for(core) + away.astype(F32)
        return mine.reshape(2, 4, n, hidden)

    def pre_grad(sent, k):
        grad_act = sent.astype(F32) + along_zl(sent).astype(F32)
        return (grad_act * slope[:, k * n : (k + 1) * n]).astype(BF)

    def y_gather(share, hold):
        near = around_y(share, True)
        far = around_y(jnp.stack([share, near]), False)
        return place4(share, near, far, y, core, 1, hold)

    def partials(gp):
        return width_contract(gp.reshape(16 * n, hidden), weight_in).reshape(4, 4, n, width)

    def chunk_of(v, k):
        return v[:, :, k * n : (k + 1) * n].reshape(16 * n, v.shape[-1])

    by_z = gather4(along_zh, out_grad, zh, 0)
    activ = gelu_parts(preact.astype(F32))[0].astype(BF)
    activ_panel = lax.all_gather(activ, "row", axis=0, tiled=True)
    pre_pair = pair2(preact, along_zl(preact), zl, 0)
    slope = gelu_parts(pre_pair.astype(F32))[1]

    low = pair2(layer_input, swap(after(layer_input, by_z), "col", 4), zh % 2, 0)
    near1 = around_x(by_z[:, n:], True)
    both1 = jnp.stack([by_z[:, n:], near1])
    og0 = gather4(along_x, by_z[:, :n], x, 0, hold=(slope, low, both1))
    mine0 = core_sum(og0)
    away0 = blocks_away(mine0, y, 1)
    input_z = pair2(low, swap(low, "col", 12), zh // 2, 0, hold=tuple(away0))
    input_z = input_z.reshape(4, tokens, width)
    far1 = around_x(after(both1, og0), False)
    og1 = place4(by_z[:, n:], near1, far1, x, core, 0, hold=(*away0, activ_panel, input_z))
    input_panel = lax.all_gather(
        after(input_z, og1), "col", axis=0, tiled=False,
        axis_index_groups=[[z * 4 + i for i in range(4)] for z in range(4)],
    )
    def out_term(k, og, *first):
        activ_x = after(activ_panel, *first).reshape(4, 4, tokens, hidden).transpose(1, 0, 2, 3)
        return token_contract(chunk_of(activ_x, k), og.reshape(16 * n, width))

    def in_term(k, gp, *first):
        return token_contract(chunk_of(after(input_panel, *first), k), gp.reshape(16 * n, hidden))

    mine1 = core_sum(og1)
    away1 = blocks_away(mine1, y, 1)
    pair0 = scatter4(along_y, mine0, away0, y, 1, hold=tuple(away1))
    gpre0 = pre_grad(pair0.astype(BF), 0)
    pair1 = scatter4(along_y, mine1, [after(v, pair0) for v in away1], y, 1, hold=(gpre0,))
    sent1 = pair1.astype(BF)
    weight_out_grad = out_term(0, og0, sent1)
    gpre1 = pre_grad(sent1, 1)
    half0 = y_gather(after(gpre0, pair1), hold=(gpre1, weight_out_grad, input_panel))
    gp0 = pair2(half0, along_core(half0), core, 1)
    part0 = partials(gp0)
    far0 = blocks_away(part0, x, 0)
    half1 = y_gather(after(gpre1, half0), hold=tuple(far0))
    gp1 = pair2(half1, along_core(half1), core, 1)
    part1 = partials(gp1)
    far1 = blocks_away(part1, x, 0)
    weight_out_grad = weight_out_grad + out_term(1, og1, *far1)
    weight_in_grad = in_term(0, gp0, *far1)
    by_x0 = scatter4(along_x, part0, far0, x, 0, hold=(*far1, weight_out_grad, weight_in_grad))
    up0 = blocks_away(by_x0, zh, 0)
    weight_in_grad = weight_in_grad + in_term(1, gp1, *up0)
    out0 = scatter4(along_zh, by_x0, up0, zh, 0).astype(BF)
    by_x1 = scatter4(along_x, part1, [after(v, by_x0) for v in far1], x, 0, hold=(weight_in_grad,))
    up1 = blocks_away(by_x1, zh, 0)
    out1 = scatter4(along_zh, by_x1, up1, zh, 0).astype(BF)
    input_grad = jnp.concatenate([out0, out1], axis=0)
    return (input_grad, weight_in_grad, weight_out_grad)


def solution(mesh):
    placed = (P("col", "row"), P("col", "row"), P("row", "col"), P("row", "col"), P("col", "row"))
    return jax.shard_map(
        local,
        mesh=mesh,
        in_specs=placed,
        out_specs=(P("col", "row"), P("row", "col"), P("col", "row")),
        check_vma=False,
    )
```

```python
import math

import jax
import jax.numpy as jnp
from jax import lax
from jax.sharding import PartitionSpec as P

BF = jnp.bfloat16
F32 = jnp.float32


def gelu_parts(h):
    c = math.sqrt(2.0 / math.pi)
    t = jnp.tanh(c * (h + 0.044715 * h * h * h))
    value = 0.5 * h * (1.0 + t)
    slope = 0.5 * (1.0 + t) + 0.5 * h * (1.0 - t * t) * c * (1.0 + 3.0 * 0.044715 * h * h)
    return (value, slope)


def token_contract(left, right):
    return lax.dot_general(left, right, (((0,), (0,)), ((), ())), preferred_element_type=F32)


def width_contract(left, right):
    return lax.dot_general(left, right, (((1,), (1,)), ((), ())), preferred_element_type=F32)


def move(v, axis, span, stride, step):
    def to(i):
        at = (i // stride) % span
        return i + (((at + step) % span) - at) * stride

    return lax.ppermute(v, axis, [(i, to(i)) for i in range(16)])


def swap(v, axis, bit):
    return lax.ppermute(v, axis, [(i, i ^ bit) for i in range(16)])


def around_x(v, first):
    def to(i):
        return i ^ (1 if (i // 16 % 2 == 0) == first else 3)

    return lax.ppermute(v, ("row", "col"), [(i, to(i)) for i in range(256)])


def around_y(v, first):
    def to(i):
        return i ^ (4 if (i % 2 == 0) == first else 12)

    return lax.ppermute(v, "row", [(i, to(i)) for i in range(16)])


def along_x(v, d):
    return move(v, "col", 4, 1, d)


def along_zh(v, d):
    return move(v, "col", 4, 4, d)


def along_y(v, d):
    return move(v, "row", 4, 4, d)


def along_zl(v):
    return move(v, "row", 2, 2, 1)


def along_core(v):
    return move(v, "row", 2, 1, 1)


STEPS = (1, -1, 2)


def put(whole, piece, at, dim):
    return lax.dynamic_update_slice_in_dim(whole, jnp.expand_dims(piece, dim), at, dim)


def take(whole, at, dim):
    return lax.dynamic_index_in_dim(whole, at, dim, keepdims=False)


def spread(own, copies, dim):
    shape = list(own.shape)
    shape.insert(dim, copies)
    return jnp.broadcast_to(jnp.expand_dims(own, dim), shape)


def gather4(shift, own, me, dim, hold=()):
    got = [(d, shift(own, d)) for d in STEPS]
    whole = after(spread(own, 4, dim), *hold)
    for d, piece in got:
        whole = put(whole, piece, (me - d) % 4, dim)
    return whole


def place4(own, near, far, me, core, dim, hold=()):
    first = 1 + 2 * core
    whole = put(after(spread(own, 4, dim), *hold), near, me ^ first, dim)
    return put(put(whole, far[0], me ^ (4 - first), dim), far[1], me ^ 2, dim)


def blocks_away(whole, me, dim):
    return [take(whole, (me + d) % 4, dim).astype(BF) for d in STEPS]


def scatter4(shift, whole, away, me, dim, hold=()):
    got = [shift(block, d) for block, d in zip(away, STEPS)]
    total = after(take(whole, me, dim), *hold)
    for piece in got:
        total = total + piece.astype(F32)
    return total


def pair2(own, other, me, dim, hold=()):
    return put(after(spread(own, 2, dim), *hold), other, 1 - me, dim)


def after(v, *others):
    return lax.optimization_barrier((v, *others))[0] if others else v


CHUNKS = 2


def local(layer_input, out_grad, preact, weight_in, weight_out):
    col, row = lax.axis_index("col"), lax.axis_index("row")
    zh, x = col // 4, col % 4
    y, zl, core = row // 4, (row // 2) % 2, row % 2
    tokens, width = out_grad.shape
    hidden = preact.shape[1]
    n = tokens // CHUNKS

    def core_sum(og):
        og5 = og.reshape(2, 2, 4, n, width)

        def grad_for(c):
            return width_contract(take(og5, c, 1).reshape(8 * n, width), weight_out)

        away = along_core(grad_for(1 - core).astype(BF))
        mine = grad_for(core) + away.astype(F32)
        return mine.reshape(2, 4, n, hidden)

    def pre_grad(sent, k):
        grad_act = sent.astype(F32) + along_zl(sent).astype(F32)
        return (grad_act * slope[:, k * n : (k + 1) * n]).astype(BF)

    def y_gather(share, hold):
        near = around_y(share, True)
        far = around_y(jnp.stack([share, near]), False)
        return place4(share, near, far, y, core, 1, hold)

    def partials(gp):
        return width_contract(gp.reshape(16 * n, hidden), weight_in).reshape(4, 4, n, width)

    def chunk_of(v, k):
        return v[:, :, k * n : (k + 1) * n].reshape(16 * n, v.shape[-1])

    by_z = gather4(along_zh, out_grad, zh, 0)
    activ = gelu_parts(preact.astype(F32))[0].astype(BF)
    activ_panel = lax.all_gather(activ, "row", axis=0, tiled=True)
    pre_pair = pair2(preact, along_zl(preact), zl, 0)
    slope = gelu_parts(pre_pair.astype(F32))[1]

    low = pair2(layer_input, swap(after(layer_input, by_z), "col", 4), zh % 2, 0)
    input_z = pair2(low, swap(low, "col", 12), zh // 2, 0)
    input_z = input_z.reshape(4, tokens, width)
    near1 = around_x(by_z[:, n:], True)
    both1 = jnp.stack([by_z[:, n:], near1])
    og0 = gather4(along_x, by_z[:, :n], x, 0, hold=(slope, input_z, both1))
    mine0 = core_sum(og0)
    away0 = blocks_away(mine0, y, 1)
    far1 = around_x(after(both1, og0), False)
    og1 = place4(by_z[:, n:], near1, far1, x, core, 0, hold=(*away0, activ_panel))
    input_panel = lax.all_gather(
        after(input_z, og1), "col", axis=0, tiled=False,
        axis_index_groups=[[z * 4 + i for i in range(4)] for z in range(4)],
    )
    def out_term(k, og, *first):
        activ_x = after(activ_panel, *first).reshape(4, 4, tokens, hidden).transpose(1, 0, 2, 3)
        return token_contract(chunk_of(activ_x, k), og.reshape(16 * n, width))

    def in_term(k, gp, *first):
        return token_contract(chunk_of(after(input_panel, *first), k), gp.reshape(16 * n, hidden))

    mine1 = core_sum(og1)
    away1 = blocks_away(mine1, y, 1)
    pair0 = scatter4(along_y, mine0, away0, y, 1, hold=tuple(away1))
    gpre0 = pre_grad(pair0.astype(BF), 0)
    pair1 = scatter4(along_y, mine1, [after(v, pair0) for v in away1], y, 1, hold=(gpre0,))
    sent1 = pair1.astype(BF)
    weight_out_grad = out_term(0, og0, sent1)
    gpre1 = pre_grad(sent1, 1)
    half0 = y_gather(after(gpre0, pair1), hold=(gpre1, weight_out_grad, input_panel))
    gp0 = pair2(half0, along_core(half0), core, 1)
    part0 = partials(gp0)
    far0 = blocks_away(part0, x, 0)
    half1 = y_gather(after(gpre1, half0), hold=tuple(far0))
    gp1 = pair2(half1, along_core(half1), core, 1)
    part1 = partials(gp1)
    far1 = blocks_away(part1, x, 0)
    weight_out_grad = weight_out_grad + out_term(1, og1, *far1)
    weight_in_grad = in_term(0, gp0, *far1)
    by_x0 = scatter4(along_x, part0, far0, x, 0, hold=(*far1, weight_out_grad, weight_in_grad))
    up0 = blocks_away(by_x0, zh, 0)
    weight_in_grad = weight_in_grad + in_term(1, gp1, *up0)
    out0 = scatter4(along_zh, by_x0, up0, zh, 0).astype(BF)
    by_x1 = scatter4(along_x, part1, [after(v, by_x0) for v in far1], x, 0, hold=(weight_in_grad,))
    up1 = blocks_away(by_x1, zh, 0)
    out1 = scatter4(along_zh, by_x1, up1, zh, 0).astype(BF)
    input_grad = jnp.concatenate([out0, out1], axis=0)
    return (input_grad, weight_in_grad, weight_out_grad)


def solution(mesh):
    placed = (P("col", "row"), P("col", "row"), P("row", "col"), P("row", "col"), P("col", "row"))
    return jax.shard_map(
        local,
        mesh=mesh,
        in_specs=placed,
        out_specs=(P("col", "row"), P("row", "col"), P("col", "row")),
        check_vma=False,
    )
```

```python
import math

import jax
import jax.numpy as jnp
from jax import lax
from jax.sharding import PartitionSpec as P

BF = jnp.bfloat16
F32 = jnp.float32


def gelu_parts(h):
    c = math.sqrt(2.0 / math.pi)
    t = jnp.tanh(c * (h + 0.044715 * h * h * h))
    value = 0.5 * h * (1.0 + t)
    slope = 0.5 * (1.0 + t) + 0.5 * h * (1.0 - t * t) * c * (1.0 + 3.0 * 0.044715 * h * h)
    return (value, slope)


def token_contract(left, right):
    return lax.dot_general(left, right, (((0,), (0,)), ((), ())), preferred_element_type=F32)


def width_contract(left, right):
    return lax.dot_general(left, right, (((1,), (1,)), ((), ())), preferred_element_type=F32)


def move(v, axis, span, stride, step):
    def to(i):
        at = (i // stride) % span
        return i + (((at + step) % span) - at) * stride

    return lax.ppermute(v, axis, [(i, to(i)) for i in range(16)])


def swap(v, axis, bit):
    return lax.ppermute(v, axis, [(i, i ^ bit) for i in range(16)])


def around_x(v, first):
    def to(i):
        return i ^ (1 if (i // 16 % 2 == 0) == first else 3)

    return lax.ppermute(v, ("row", "col"), [(i, to(i)) for i in range(256)])


def around_y(v, first):
    def to(i):
        return i ^ (4 if (i % 2 == 0) == first else 12)

    return lax.ppermute(v, "row", [(i, to(i)) for i in range(16)])


def along_x(v, d):
    return move(v, "col", 4, 1, d)


def along_zh(v, d):
    return move(v, "col", 4, 4, d)


def along_y(v, d):
    return move(v, "row", 4, 4, d)


def along_zl(v):
    return move(v, "row", 2, 2, 1)


def along_core(v):
    return move(v, "row", 2, 1, 1)


STEPS = (1, -1, 2)


def put(whole, piece, at, dim):
    return lax.dynamic_update_slice_in_dim(whole, jnp.expand_dims(piece, dim), at, dim)


def take(whole, at, dim):
    return lax.dynamic_index_in_dim(whole, at, dim, keepdims=False)


def spread(own, copies, dim):
    shape = list(own.shape)
    shape.insert(dim, copies)
    return jnp.broadcast_to(jnp.expand_dims(own, dim), shape)


def gather4(shift, own, me, dim, hold=()):
    got = [(d, shift(own, d)) for d in STEPS]
    whole = after(spread(own, 4, dim), *hold)
    for d, piece in got:
        whole = put(whole, piece, (me - d) % 4, dim)
    return whole


def place4(own, near, far, me, core, dim, hold=()):
    first = 1 + 2 * core
    whole = put(after(spread(own, 4, dim), *hold), near, me ^ first, dim)
    return put(put(whole, far[0], me ^ (4 - first), dim), far[1], me ^ 2, dim)


def blocks_away(whole, me, dim):
    return [take(whole, (me + d) % 4, dim).astype(BF) for d in STEPS]


def scatter4(shift, whole, away, me, dim, hold=()):
    got = [shift(block, d) for block, d in zip(away, STEPS)]
    total = after(take(whole, me, dim), *hold)
    for piece in got:
        total = total + piece.astype(F32)
    return total


def pair2(own, other, me, dim, hold=()):
    return put(after(spread(own, 2, dim), *hold), other, 1 - me, dim)


def after(v, *others):
    return lax.optimization_barrier((v, *others))[0] if others else v


CHUNKS = 2


def local(layer_input, out_grad, preact, weight_in, weight_out):
    col, row = lax.axis_index("col"), lax.axis_index("row")
    zh, x = col // 4, col % 4
    y, zl, core = row // 4, (row // 2) % 2, row % 2
    tokens, width = out_grad.shape
    hidden = preact.shape[1]
    n = tokens // CHUNKS

    def core_sum(og):
        og5 = og.reshape(2, 2, 4, n, width)

        def grad_for(c):
            return width_contract(take(og5, c, 1).reshape(8 * n, width), weight_out)

        away = along_core(grad_for(1 - core).astype(BF))
        mine = grad_for(core) + away.astype(F32)
        return mine.reshape(2, 4, n, hidden)

    def pre_grad(sent, k):
        grad_act = sent.astype(F32) + along_zl(sent).astype(F32)
        return (grad_act * slope[:, k * n : (k + 1) * n]).astype(BF)

    def y_gather(share, hold):
        near = around_y(share, True)
        far = around_y(jnp.stack([share, near]), False)
        return place4(share, near, far, y, core, 1, hold)

    def partials(gp):
        return width_contract(gp.reshape(16 * n, hidden), weight_in).reshape(4, 4, n, width)

    def chunk_of(v, k):
        return v[:, :, k * n : (k + 1) * n].reshape(16 * n, v.shape[-1])

    by_z = gather4(along_zh, out_grad, zh, 0)
    activ = gelu_parts(preact.astype(F32))[0].astype(BF)
    activ_panel = lax.all_gather(activ, "row", axis=0, tiled=True)
    pre_pair = pair2(preact, along_zl(preact), zl, 0)
    slope = gelu_parts(pre_pair.astype(F32))[1]

    low = pair2(layer_input, swap(after(layer_input, by_z), "col", 4), zh % 2, 0)
    near1 = around_x(by_z[:, n:], True)
    both1 = jnp.stack([by_z[:, n:], near1])
    og0 = gather4(along_x, by_z[:, :n], x, 0, hold=(slope, low, both1))
    mine0 = core_sum(og0)
    away0 = blocks_away(mine0, y, 1)
    far1 = around_x(after(both1, og0), False)
    og1 = place4(by_z[:, n:], near1, far1, x, core, 0, hold=(*away0, activ_panel))
    def out_term(k, og, *first):
        activ_x = after(activ_panel, *first).reshape(4, 4, tokens, hidden).transpose(1, 0, 2, 3)
        return token_contract(chunk_of(activ_x, k), og.reshape(16 * n, width))

    def in_term(k, gp, *first):
        return token_contract(chunk_of(after(input_panel, *first), k), gp.reshape(16 * n, hidden))

    mine1 = core_sum(og1)
    away1 = blocks_away(mine1, y, 1)
    input_z = pair2(low, swap(after(low, og1), "col", 12), zh // 2, 0, hold=tuple(away1))
    input_z = input_z.reshape(4, tokens, width)
    input_near = around_x(input_z, True)
    input_far = around_x(jnp.stack([input_z, input_near]), False)
    input_panel = place4(input_z, input_near, input_far, x, core, 0)
    pair0 = scatter4(along_y, mine0, away0, y, 1, hold=tuple(away1))
    gpre0 = pre_grad(pair0.astype(BF), 0)
    pair1 = scatter4(along_y, mine1, [after(v, pair0) for v in away1], y, 1, hold=(gpre0,))
    sent1 = pair1.astype(BF)
    weight_out_grad = out_term(0, og0, sent1)
    gpre1 = pre_grad(sent1, 1)
    half0 = y_gather(after(gpre0, pair1), hold=(gpre1, weight_out_grad, input_panel))
    gp0 = pair2(half0, along_core(half0), core, 1)
    part0 = partials(gp0)
    far0 = blocks_away(part0, x, 0)
    half1 = y_gather(after(gpre1, half0), hold=tuple(far0))
    gp1 = pair2(half1, along_core(half1), core, 1)
    part1 = partials(gp1)
    far1 = blocks_away(part1, x, 0)
    weight_out_grad = weight_out_grad + out_term(1, og1, *far1)
    weight_in_grad = in_term(0, gp0, *far1)
    by_x0 = scatter4(along_x, part0, far0, x, 0, hold=(*far1, weight_out_grad, weight_in_grad))
    up0 = blocks_away(by_x0, zh, 0)
    weight_in_grad = weight_in_grad + in_term(1, gp1, *up0)
    out0 = scatter4(along_zh, by_x0, up0, zh, 0).astype(BF)
    by_x1 = scatter4(along_x, part1, [after(v, by_x0) for v in far1], x, 0, hold=(weight_in_grad,))
    up1 = blocks_away(by_x1, zh, 0)
    out1 = scatter4(along_zh, by_x1, up1, zh, 0).astype(BF)
    input_grad = jnp.concatenate([out0, out1], axis=0)
    return (input_grad, weight_in_grad, weight_out_grad)


def solution(mesh):
    placed = (P("col", "row"), P("col", "row"), P("row", "col"), P("row", "col"), P("col", "row"))
    return jax.shard_map(
        local,
        mesh=mesh,
        in_specs=placed,
        out_specs=(P("col", "row"), P("row", "col"), P("col", "row")),
        check_vma=False,
    )
```

```python
import math

import jax
import jax.numpy as jnp
from jax import lax
from jax.sharding import PartitionSpec as P

BF = jnp.bfloat16
F32 = jnp.float32


def gelu_parts(h):
    c = math.sqrt(2.0 / math.pi)
    t = jnp.tanh(c * (h + 0.044715 * h * h * h))
    value = 0.5 * h * (1.0 + t)
    slope = 0.5 * (1.0 + t) + 0.5 * h * (1.0 - t * t) * c * (1.0 + 3.0 * 0.044715 * h * h)
    return (value, slope)


def token_contract(left, right):
    return lax.dot_general(left, right, (((0,), (0,)), ((), ())), preferred_element_type=F32)


def width_contract(left, right):
    return lax.dot_general(left, right, (((1,), (1,)), ((), ())), preferred_element_type=F32)


def move(v, axis, span, stride, step):
    def to(i):
        at = (i // stride) % span
        return i + (((at + step) % span) - at) * stride

    return lax.ppermute(v, axis, [(i, to(i)) for i in range(16)])


def swap(v, axis, bit):
    return lax.ppermute(v, axis, [(i, i ^ bit) for i in range(16)])


def around_x(v, first):
    def to(i):
        return i ^ (1 if (i // 16 % 2 == 0) == first else 3)

    return lax.ppermute(v, ("row", "col"), [(i, to(i)) for i in range(256)])


def around_y(v, first):
    def to(i):
        return i ^ (4 if (i % 2 == 0) == first else 12)

    return lax.ppermute(v, "row", [(i, to(i)) for i in range(16)])


def along_x(v, d):
    return move(v, "col", 4, 1, d)


def along_zh(v, d):
    return move(v, "col", 4, 4, d)


def along_y(v, d):
    return move(v, "row", 4, 4, d)


def along_zl(v):
    return move(v, "row", 2, 2, 1)


def along_core(v):
    return move(v, "row", 2, 1, 1)


STEPS = (1, -1, 2)


def put(whole, piece, at, dim):
    return lax.dynamic_update_slice_in_dim(whole, jnp.expand_dims(piece, dim), at, dim)


def take(whole, at, dim):
    return lax.dynamic_index_in_dim(whole, at, dim, keepdims=False)


def spread(own, copies, dim):
    shape = list(own.shape)
    shape.insert(dim, copies)
    return jnp.broadcast_to(jnp.expand_dims(own, dim), shape)


def gather4(shift, own, me, dim, hold=()):
    got = [(d, shift(own, d)) for d in STEPS]
    whole = after(spread(own, 4, dim), *hold)
    for d, piece in got:
        whole = put(whole, piece, (me - d) % 4, dim)
    return whole


def place4(own, near, far, me, core, dim, hold=()):
    first = 1 + 2 * core
    whole = put(after(spread(own, 4, dim), *hold), near, me ^ first, dim)
    return put(put(whole, far[0], me ^ (4 - first), dim), far[1], me ^ 2, dim)


def blocks_away(whole, me, dim):
    return [take(whole, (me + d) % 4, dim).astype(BF) for d in STEPS]


def scatter4(shift, whole, away, me, dim, hold=()):
    got = [shift(block, d) for block, d in zip(away, STEPS)]
    total = after(take(whole, me, dim), *hold)
    for piece in got:
        total = total + piece.astype(F32)
    return total


def pair2(own, other, me, dim, hold=()):
    return put(after(spread(own, 2, dim), *hold), other, 1 - me, dim)


def after(v, *others):
    return lax.optimization_barrier((v, *others))[0] if others else v


CHUNKS = 2


def local(layer_input, out_grad, preact, weight_in, weight_out):
    col, row = lax.axis_index("col"), lax.axis_index("row")
    zh, x = col // 4, col % 4
    y, zl, core = row // 4, (row // 2) % 2, row % 2
    tokens, width = out_grad.shape
    hidden = preact.shape[1]
    n = tokens // CHUNKS

    def core_sum(og):
        og5 = og.reshape(2, 2, 4, n, width)

        def grad_for(c):
            return width_contract(take(og5, c, 1).reshape(8 * n, width), weight_out)

        away = along_core(grad_for(1 - core).astype(BF))
        mine = grad_for(core) + away.astype(F32)
        return mine.reshape(2, 4, n, hidden)

    def pre_grad(sent, k):
        grad_act = sent.astype(F32) + along_zl(sent).astype(F32)
        return (grad_act * slope[:, k * n : (k + 1) * n]).astype(BF)

    def y_gather(share, hold):
        near = around_y(share, True)
        far = around_y(jnp.stack([share, near]), False)
        return place4(share, near, far, y, core, 1, hold)

    def partials(gp):
        return width_contract(gp.reshape(16 * n, hidden), weight_in).reshape(4, 4, n, width)

    def chunk_of(v, k):
        return v[:, :, k * n : (k + 1) * n].reshape(16 * n, v.shape[-1])

    by_z = gather4(along_zh, out_grad, zh, 0)
    activ = gelu_parts(preact.astype(F32))[0].astype(BF)
    activ_panel = lax.all_gather(activ, "row", axis=0, tiled=True)
    pre_pair = pair2(preact, along_zl(preact), zl, 0)
    slope = gelu_parts(pre_pair.astype(F32))[1]

    low = pair2(layer_input, swap(after(layer_input, by_z), "col", 4), zh % 2, 0)
    near1 = around_x(by_z[:, n:], True)
    both1 = jnp.stack([by_z[:, n:], near1])
    og0 = gather4(along_x, by_z[:, :n], x, 0, hold=(slope, low, both1))
    mine0 = core_sum(og0)
    away0 = blocks_away(mine0, y, 1)
    far1 = around_x(after(both1, og0), False)
    og1 = place4(by_z[:, n:], near1, far1, x, core, 0, hold=(*away0, activ_panel))
    def out_term(k, og, *first):
        activ_x = after(activ_panel, *first).reshape(4, 4, tokens, hidden).transpose(1, 0, 2, 3)
        return token_contract(chunk_of(activ_x, k), og.reshape(16 * n, width))

    def in_term(k, gp, *first):
        return token_contract(chunk_of(after(input_panel, *first), k), gp.reshape(16 * n, hidden))

    mine1 = core_sum(og1)
    away1 = blocks_away(mine1, y, 1)
    pair0 = scatter4(along_y, mine0, away0, y, 1, hold=tuple(away1))
    gpre0 = pre_grad(pair0.astype(BF), 0)
    input_z = pair2(low, swap(after(low, og1), "col", 12), zh // 2, 0, hold=(gpre0,))
    input_z = input_z.reshape(4, tokens, width)
    input_near = around_x(input_z, True)
    input_far = around_x(jnp.stack([input_z, input_near]), False)
    input_panel = place4(input_z, input_near, input_far, x, core, 0)
    pair1 = scatter4(along_y, mine1, [after(v, pair0) for v in away1], y, 1, hold=(gpre0,))
    sent1 = pair1.astype(BF)
    weight_out_grad = out_term(0, og0, sent1)
    gpre1 = pre_grad(sent1, 1)
    half0 = y_gather(after(gpre0, pair1), hold=(gpre1, weight_out_grad, input_panel))
    gp0 = pair2(half0, along_core(half0), core, 1)
    part0 = partials(gp0)
    far0 = blocks_away(part0, x, 0)
    half1 = y_gather(after(gpre1, half0), hold=tuple(far0))
    gp1 = pair2(half1, along_core(half1), core, 1)
    part1 = partials(gp1)
    far1 = blocks_away(part1, x, 0)
    weight_out_grad = weight_out_grad + out_term(1, og1, *far1)
    weight_in_grad = in_term(0, gp0, *far1)
    by_x0 = scatter4(along_x, part0, far0, x, 0, hold=(*far1, weight_out_grad, weight_in_grad))
    up0 = blocks_away(by_x0, zh, 0)
    weight_in_grad = weight_in_grad + in_term(1, gp1, *up0)
    out0 = scatter4(along_zh, by_x0, up0, zh, 0).astype(BF)
    by_x1 = scatter4(along_x, part1, [after(v, by_x0) for v in far1], x, 0, hold=(weight_in_grad,))
    up1 = blocks_away(by_x1, zh, 0)
    out1 = scatter4(along_zh, by_x1, up1, zh, 0).astype(BF)
    input_grad = jnp.concatenate([out0, out1], axis=0)
    return (input_grad, weight_in_grad, weight_out_grad)


def solution(mesh):
    placed = (P("col", "row"), P("col", "row"), P("row", "col"), P("row", "col"), P("col", "row"))
    return jax.shard_map(
        local,
        mesh=mesh,
        in_specs=placed,
        out_specs=(P("col", "row"), P("row", "col"), P("col", "row")),
        check_vma=False,
    )
```
